512 devices in a mesh: col: 16 (over y, x_hi, core), blk: 32 (over z, x_lo).
Axes of the slice: x: 4 (x_hi: 2, x_lo: 2; x = x_hi * 2 + x_lo), y: 4, z: 16, core: 2. Of those that a mesh axis runs over, the one named last changes fastest.
Arguments:
- tokens: bfloat16 [2048, 6144], P('blk', 'col'), may hold values from -6 to 6
- route_ids: int32 [2048, 2], P('blk'), may hold values from 0 to 7, as said below
- route_gates: float32 [2048, 2], P('blk'), may hold values from 0.2 to 1
- gate_weight: bfloat16 [2, 6144, 16384], P(None, 'col', 'blk'), may hold values from -0.078125 to 0.078125
- up_weight: bfloat16 [2, 6144, 16384], P(None, 'col', 'blk'), may hold values from -0.078125 to 0.078125
- gate_scale: float32 [2, 48, 128], P(None, 'col', 'blk'), may hold values from 0.5 to 2
- up_scale: float32 [2, 48, 128], P(None, 'col', 'blk'), may hold values from 0.5 to 2
- down_weight: bfloat16 [2, 16384, 6144], P(None, 'blk', 'col'), may hold values from -0.046875 to 0.046875
- down_scale: float32 [2, 128, 48], P(None, 'blk', 'col'), may hold values from 0.5 to 2
Outputs:
- mixed: bfloat16 [2048, 6144], P('blk', 'col')
The draws below stay inside these ranges and needn't reach their ends.
Inputs may be any that keep to these rules, and one draw needn't show every extreme that they name: `route_ids`: in each aligned block of 64 rows the two ids of a row differ, and each expert below 2 is named by at most 20 rows of the block; in every block one of them is named by exactly 20 rows.
All inputs are finite; a program needn't handle non-finite values.
Results may differ from the reference program's by a relative error of at most 0.0049.
Values may be sent and summed in bfloat16 or wider, within the bound.
No kernel may reach another device: no remote copies, remote signals or barrier semaphores. Data moves between devices by JAX's collectives and lax.ppermute only.
A program may use at most 64 MiB of HBM per device.

```python
import math
import jax
import jax.numpy as jnp
from jax import lax

D = 6144
FF = 16384
EXPERTS = 8
TOP = 2
EXPW = 2
SB = 128
TOK_DEV = 64
CAP = 20
TOKENS = 2048
N_COL = 16
N_BLK = 32


def draw_route_ids(key, part):
    key = jax.random.fold_in(key, 7)
    blocks = TOKENS // TOK_DEV
    keys = jax.random.split(key, 5)
    full_expert = jax.random.randint(keys[0], (blocks, 1), 0, EXPW)
    other_counts = jax.random.randint(keys[1], (blocks, EXPW), 1, CAP + 1)
    window = jnp.arange(EXPW, dtype=jnp.int32)[None, :]
    window_counts = jnp.where(window == full_expert, CAP, other_counts).astype(jnp.int32)
    remaining = 2 * TOK_DEV - jnp.sum(window_counts, axis=1, keepdims=True)
    spare = EXPERTS - EXPW
    ranking = jax.vmap(lambda sub: jax.random.permutation(sub, spare))(jax.random.split(keys[2], blocks))
    rest_counts = remaining // spare + (ranking < remaining % spare).astype(jnp.int32)
    counts = jnp.concatenate([window_counts, rest_counts.astype(jnp.int32)], axis=1)
    bounds = jnp.cumsum(counts, axis=1)
    position = jnp.arange(2 * TOK_DEV, dtype=jnp.int32)
    labels = jnp.sum((position[None, :, None] >= bounds[:, None, :]).astype(jnp.int32), axis=2)
    pairs = jnp.transpose(labels.reshape(blocks, 2, TOK_DEV), (0, 2, 1))
    ordering = jax.vmap(lambda sub: jax.random.permutation(sub, TOK_DEV))(jax.random.split(keys[3], blocks))
    pairs = jnp.take_along_axis(pairs, ordering[:, :, None], axis=1)
    flipped = jax.random.randint(keys[4], (blocks, TOK_DEV, 1), 0, 2)
    pairs = jnp.where(flipped == 1, pairs[:, :, ::-1], pairs)
    return pairs.reshape(TOKENS, 2).astype(jnp.int32)


def levels(key, shape, shards, smallest, top_value):
    def one(axis_at, blocks):
        heights = jax.random.uniform(jax.random.fold_in(jax.random.fold_in(key, 6), axis_at), (blocks,), jnp.float32, smallest / len(shards), top_value / len(shards))
        return jnp.repeat(jnp.exp(heights), shape[axis_at] // blocks).reshape((-1,) + (1,) * (len(shape) - axis_at - 1))

    level = one(*shards[0])
    for cut in shards[1:]:
        level = level * one(*cut)
    return level


def noise(stream_key, shape, scale, most, cuts=(), kind=jnp.bfloat16):
    values = jax.random.normal(stream_key, shape, jnp.float32) * scale
    if len(cuts) > 0:
        values = levels(stream_key, shape, cuts, -0.22, 0.18) * values
    return jnp.clip(values, min=-most, max=most).astype(kind)


def setup_inputs(seed: int = 0) -> dict:
    seeds = jax.random.split(jax.random.key(seed), 10)
    tokens = noise(seeds[0], (TOKENS, D), 1.0, 6.0, ((0, 32), (1, 16)))
    route_ids = draw_route_ids(jax.random.fold_in(seeds[9], 71), 0)
    route_gates = jnp.clip(0.2 + 0.8 * jax.random.uniform(seeds[2], (TOKENS, TOP), jnp.float32) ** levels(seeds[2], (TOKENS, TOP), ((0, 32),), -0.2, 0.2), 0.2, 1.0)
    gate_weight = noise(seeds[3], (EXPW, D, FF), D ** -0.5, 0.078125, ((1, 16), (2, 32)))
    up_weight = noise(seeds[4], (EXPW, D, FF), D ** -0.5, 0.078125, ((1, 16), (2, 32)))
    gate_scale = jnp.clip(jnp.exp(math.log(2.0) - 1.3862944 * jax.random.uniform(seeds[5], (EXPW, D // SB, FF // SB), jnp.float32) ** levels(seeds[5], (EXPW, D // SB, FF // SB), ((1, 16), (2, 32)), -0.2, 0.2)), 0.5, 2.0)
    up_scale = jnp.clip(jnp.exp(math.log(2.0) - 1.3862944 * jax.random.uniform(seeds[6], (EXPW, D // SB, FF // SB), jnp.float32) ** levels(seeds[6], (EXPW, D // SB, FF // SB), ((1, 16), (2, 32)), -0.2, 0.2)), 0.5, 2.0)
    down_weight = noise(seeds[7], (EXPW, FF, D), FF ** -0.5, 0.046875, ((1, 32), (2, 16)))
    down_scale = jnp.clip(jnp.exp(math.log(2.0) - 1.3862944 * jax.random.uniform(seeds[8], (EXPW, FF // SB, D // SB), jnp.float32) ** levels(seeds[8], (EXPW, FF // SB, D // SB), ((1, 32), (2, 16)), -0.2, 0.2)), 0.5, 2.0)
    return {"tokens": tokens, "route_ids": route_ids, "route_gates": route_gates, "gate_weight": gate_weight, "up_weight": up_weight, "gate_scale": gate_scale, "up_scale": up_scale, "down_weight": down_weight, "down_scale": down_scale}


def dispatch(route_ids, route_gates):
    expert_ids = jnp.arange(EXPW, dtype=jnp.int32)
    matches = route_ids[:, :, None] == expert_ids[None, None, :]
    chosen = jnp.any(matches, axis=1)
    combine_weights = jnp.sum(jnp.where(matches, route_gates[:, :, None], jnp.zeros((), route_gates.dtype)), axis=1)
    slot_index = jnp.cumsum(chosen.astype(jnp.int32), axis=0) - 1
    onehot = chosen[:, :, None] & (slot_index[:, :, None] == jnp.arange(CAP, dtype=jnp.int32)[None, None, :])
    return onehot, combine_weights


def blocked(row_block, weight, scale):
    square = weight.shape[1] // scale.shape[1]
    running = jnp.zeros(row_block.shape[:2] + (weight.shape[2],), jnp.float32)
    for position in range(scale.shape[1]):
        offset = position * square
        product = jnp.einsum('rek,ekf->ref', row_block[:, :, offset:offset + square].astype(jnp.float32),
                             weight[:, offset:offset + square, :].astype(jnp.float32),
                             precision=lax.Precision.HIGHEST)
        running = running + product * jnp.repeat(scale[:, position, :], square, axis=-1)[None, :, :]
    return running


def reference(tokens, route_ids, route_gates, gate_weight, up_weight, gate_scale, up_scale, down_weight, down_scale):
    block_ids = route_ids.reshape(N_BLK, TOK_DEV, TOP)
    block_gates = route_gates.reshape(N_BLK, TOK_DEV, TOP)
    onehot, combine_weights = jax.vmap(dispatch)(block_ids, block_gates)
    token_blocks = tokens.reshape(N_BLK, TOK_DEV, D).astype(jnp.float32)
    dispatched = jnp.einsum('btec,btd->bced', onehot.astype(jnp.float32), token_blocks,
                            precision=lax.Precision.HIGHEST).astype(jnp.bfloat16)
    dispatched = dispatched.reshape(N_BLK * CAP, EXPW, D)
    features = D // N_COL
    scale_cols = features // SB
    gate = jnp.zeros((N_BLK * CAP, EXPW, FF), jnp.float32)
    up = jnp.zeros((N_BLK * CAP, EXPW, FF), jnp.float32)
    for group_index in range(N_COL):
        lower_feat = group_index * features
        lower_scale = group_index * scale_cols
        piece_rows = dispatched[:, :, lower_feat:lower_feat + features]
        gate = gate + blocked(piece_rows, gate_weight[:, lower_feat:lower_feat + features, :],
                              gate_scale[:, lower_scale:lower_scale + scale_cols, :])
        up = up + blocked(piece_rows, up_weight[:, lower_feat:lower_feat + features, :],
                          up_scale[:, lower_scale:lower_scale + scale_cols, :])
    hidden = (jax.nn.silu(gate) * up).astype(jnp.bfloat16)
    units = FF // N_BLK
    scale_rows = units // SB
    expert_out = jnp.zeros((N_BLK * CAP, EXPW, D), jnp.float32)
    for group_index in range(N_BLK):
        lower_unit = group_index * units
        lower_scale = group_index * scale_rows
        expert_out = expert_out + blocked(hidden[:, :, lower_unit:lower_unit + units],
                                          down_weight[:, lower_unit:lower_unit + units, :],
                                          down_scale[:, lower_scale:lower_scale + scale_rows, :])
    expert_out = expert_out.reshape(N_BLK, CAP, EXPW, D)
    combine = onehot.astype(jnp.float32) * combine_weights[:, :, :, None]
    mixed = jnp.einsum('btec,bced->btd', combine, expert_out, precision=lax.Precision.HIGHEST)
    return mixed.reshape(TOKENS, D).astype(jnp.bfloat16)
```

```python
import jax
import jax.numpy as jnp
from jax import lax
from jax.sharding import Mesh, PartitionSpec as P

EXPW = 2
CAP = 20
SB = 128
COL = ("y", "xh", "core")
BLK = ("zh", "zl", "xl")
SIZES = {"y": 4, "xh": 2, "core": 2, "zh": 4, "zl": 4, "xl": 2}
F32 = jnp.float32
BF16 = jnp.bfloat16


def dispatch(route_ids, route_gates):
    expert_ids = jnp.arange(EXPW, dtype=jnp.int32)
    matches = route_ids[:, :, None] == expert_ids[None, None, :]
    chosen = jnp.any(matches, axis=1)
    combine_weights = jnp.sum(
        jnp.where(matches, route_gates[:, :, None], jnp.zeros((), route_gates.dtype)), axis=1
    )
    slot_index = jnp.cumsum(chosen.astype(jnp.int32), axis=0) - 1
    onehot = chosen[:, :, None] & (
        slot_index[:, :, None] == jnp.arange(CAP, dtype=jnp.int32)[None, None, :]
    )
    return (onehot, combine_weights)


def swap(value):
    return lax.ppermute(value, "core", [(0, 1), (1, 0)])


def gather(value, axes, count):
    return lax.all_to_all(
        jnp.broadcast_to(value[None], (count,) + value.shape), axes, 0, 0, tiled=True
    )


def exchange_sum(value, axes):
    received = lax.all_to_all(value, axes, 0, 0, tiled=True)
    return jnp.sum(received.astype(F32), axis=0)


def blocked(rows, weight, scale):
    running = jnp.zeros((rows.shape[0], weight.shape[1]), F32)
    for position in range(scale.shape[0]):
        cut = slice(position * SB, (position + 1) * SB)
        product = jnp.dot(rows[:, cut], weight[cut], preferred_element_type=F32)
        running = running + product * jnp.repeat(scale[position], SB)[None, :]
    return running


def both_cores(array, core, axis):
    own = lax.dynamic_index_in_dim(array, core, 0, keepdims=False)
    other = swap(lax.dynamic_index_in_dim(array, 1 - core, 0, keepdims=False))
    first = jnp.where(core == 0, own, other)
    second = jnp.where(core == 0, other, own)
    return jnp.concatenate([first, second], axis=axis)


def shards(
    tokens,
    route_ids,
    route_gates,
    gate_weight,
    up_weight,
    gate_scale,
    up_scale,
    down_weight,
    down_scale,
):
    core = lax.axis_index("core")
    width = tokens.shape[1]
    hidden_width = gate_weight.shape[2]
    other_tokens = swap(tokens)
    tokens2 = jnp.concatenate(
        [
            jnp.where(core == 0, tokens, other_tokens),
            jnp.where(core == 0, other_tokens, tokens),
        ],
        axis=1,
    )
    onehot, combine_weights = dispatch(route_ids, route_gates)
    mine = lax.dynamic_index_in_dim(onehot, core, 1, keepdims=False)
    slot_rows = jnp.einsum(
        "tc,td->cd", mine.astype(BF16), tokens2, preferred_element_type=F32
    ).astype(BF16)
    portion = gather(slot_rows, "zh", 4).reshape(4 * CAP, 2 * width)
    portion = gather(portion, ("zl", "xl"), 8).reshape(32 * CAP, 2 * width)

    gate_up_weight = both_cores(jnp.concatenate([gate_weight, up_weight], axis=2), core, 0)
    gate_up_scale = both_cores(jnp.concatenate([gate_scale, up_scale], axis=2), core, 0)
    down_both = both_cores(down_weight, core, 1)
    down_scale_both = both_cores(down_scale, core, 1)

    partial_sums = blocked(portion, gate_up_weight, gate_up_scale).astype(BF16)
    summed = exchange_sum(partial_sums.reshape(8, 4 * CAP, 2 * hidden_width), ("y", "xh"))
    hidden = (jax.nn.silu(summed[:, :hidden_width]) * summed[:, hidden_width:]).astype(BF16)
    hidden = gather(hidden, ("y", "xh"), 8).reshape(32 * CAP, hidden_width)
    down = blocked(hidden, down_both, down_scale_both).astype(BF16)
    down = exchange_sum(down.reshape(8, 4 * CAP, 2 * width), ("zl", "xl")).astype(BF16)
    expert_out = exchange_sum(down.reshape(4, CAP, 2 * width), "zh")

    kept = lax.dynamic_slice_in_dim(expert_out, core * width, width, 1)
    given = swap(lax.dynamic_slice_in_dim(expert_out, (1 - core) * width, width, 1))
    first = jnp.where(core == 0, kept, given)
    second = jnp.where(core == 0, given, kept)
    combine = onehot.astype(F32) * combine_weights[:, :, None]
    mixed = jnp.dot(combine[:, 0], first, precision=lax.Precision.HIGHEST) + jnp.dot(
        combine[:, 1], second, precision=lax.Precision.HIGHEST
    )
    return mixed.astype(BF16)


def solution(mesh):
    parts = Mesh(mesh.devices.reshape(tuple(SIZES.values())), tuple(SIZES))
    in_specs = (
        P(BLK, COL),
        P(BLK, None),
        P(BLK, None),
        P(None, COL, BLK),
        P(None, COL, BLK),
        P(None, COL, BLK),
        P(None, COL, BLK),
        P(None, BLK, COL),
        P(None, BLK, COL),
    )
    return jax.shard_map(
        shards, mesh=parts, in_specs=in_specs, out_specs=P(BLK, COL), check_vma=False
    )
```

```python
import jax
import jax.numpy as jnp
from jax import lax
from jax.sharding import Mesh, PartitionSpec as P

EXPW = 2
CAP = 20
SB = 128
COL = ("y", "xh", "core")
BLK = ("zh", "zl", "xl")
SIZES = {"y": 4, "xh": 2, "core": 2, "zh": 8, "zl": 2, "xl": 2}
ZH = SIZES["zh"]
NEAR = SIZES["zl"] * SIZES["xl"]
GROUP = SIZES["y"] * SIZES["xh"]
F32 = jnp.float32
BF16 = jnp.bfloat16
SHIFT = 64.0


def dispatch(route_ids, route_gates):
    expert_ids = jnp.arange(EXPW, dtype=jnp.int32)
    matches = route_ids[:, :, None] == expert_ids[None, None, :]
    chosen = jnp.any(matches, axis=1)
    combine_weights = jnp.sum(
        jnp.where(matches, route_gates[:, :, None], jnp.zeros((), route_gates.dtype)), axis=1
    )
    slot_index = jnp.cumsum(chosen.astype(jnp.int32), axis=0) - 1
    onehot = chosen[:, :, None] & (
        slot_index[:, :, None] == jnp.arange(CAP, dtype=jnp.int32)[None, None, :]
    )
    return (onehot, combine_weights)


def swap(value):
    return lax.ppermute(value, "core", [(0, 1), (1, 0)])


def trade(value, axes):
    return lax.all_to_all(value, axes, 0, 0, tiled=True)


def gather(value, axes, count):
    return trade(jnp.broadcast_to(value[None], (count,) + value.shape), axes)


def blocked(rows, weight, scale):
    running = jnp.zeros((rows.shape[0], weight.shape[1]), F32)
    for position in range(scale.shape[0]):
        cut = slice(position * SB, (position + 1) * SB)
        product = jnp.dot(rows[:, cut], weight[cut], preferred_element_type=F32)
        running = running + product * jnp.repeat(scale[position], SB)[None, :]
    return running


def both_cores(array, core, axis):
    own = lax.dynamic_index_in_dim(array, core, 0, keepdims=False)
    other = swap(lax.dynamic_index_in_dim(array, 1 - core, 0, keepdims=False))
    first = jnp.where(core == 0, own, other)
    second = jnp.where(core == 0, other, own)
    return jnp.concatenate([first, second], axis=axis)


def shards(
    tokens,
    route_ids,
    route_gates,
    gate_weight,
    up_weight,
    gate_scale,
    up_scale,
    down_weight,
    down_scale,
):
    core = lax.axis_index("core")
    width = tokens.shape[1]
    hidden_width = gate_weight.shape[2]
    near_rows = ZH * CAP
    rows = NEAR * near_rows
    onehot, combine_weights = dispatch(route_ids, route_gates)
    slot_rows = jnp.einsum(
        "tec,td->ecd", onehot.astype(BF16), tokens, preferred_element_type=F32
    ).astype(BF16)
    far = jnp.broadcast_to(slot_rows[None], (ZH, 2, CAP, width)).reshape(2 * ZH, CAP, width)
    far = trade(far, ("zh", "core")).reshape(ZH, 2, CAP, width)
    far = far.transpose(0, 2, 1, 3).reshape(near_rows, 2 * width)
    portion = gather(far, ("zl", "xl"), NEAR).reshape(rows, 2 * width)

    gate_up_weight = both_cores(jnp.concatenate([gate_weight, up_weight], axis=2), core, 0)
    gate_up_scale = both_cores(jnp.concatenate([gate_scale, up_scale], axis=2), core, 0)
    down_both = both_cores(down_weight, core, 1)
    down_scale_both = both_cores(down_scale, core, 1)

    partial_sums = (blocked(portion, gate_up_weight, gate_up_scale) * SHIFT).astype(jnp.float16)
    received = trade(partial_sums.reshape(GROUP, rows // GROUP, 2 * hidden_width), ("y", "xh"))
    summed = jnp.sum(received.astype(F32), axis=0) * (1.0 / SHIFT)
    hidden = (jax.nn.silu(summed[:, :hidden_width]) * summed[:, hidden_width:]).astype(BF16)
    hidden = gather(hidden, ("y", "xh"), GROUP).reshape(rows, hidden_width)
    down = blocked(hidden, down_both, down_scale_both).astype(BF16)
    down = trade(down.reshape(NEAR, near_rows, 2 * width), ("zl", "xl"))
    down = jnp.sum(down.astype(F32), axis=0).astype(BF16)
    down = down.reshape(ZH, CAP, 2, width).transpose(0, 2, 1, 3).reshape(2 * ZH, CAP, width)
    down = trade(down, ("zh", "core")).reshape(ZH, 2, CAP, width)
    expert_out = jnp.sum(down.astype(F32), axis=0)

    combine = onehot.astype(F32) * combine_weights[:, :, None]
    mixed = jnp.einsum("tec,ecd->td", combine, expert_out, precision=lax.Precision.HIGHEST)
    return mixed.astype(BF16)


def solution(mesh):
    parts = Mesh(mesh.devices.reshape(tuple(SIZES.values())), tuple(SIZES))
    in_specs = (
        P(BLK, COL),
        P(BLK, None),
        P(BLK, None),
        P(None, COL, BLK),
        P(None, COL, BLK),
        P(None, COL, BLK),
        P(None, COL, BLK),
        P(None, BLK, COL),
        P(None, BLK, COL),
    )
    return jax.shard_map(
        shards, mesh=parts, in_specs=in_specs, out_specs=P(BLK, COL), check_vma=False
    )
```

```python
import jax
import jax.numpy as jnp
from jax import lax
from jax.experimental import pallas as pl
from jax.experimental.pallas import tpu as pltpu
from jax.sharding import Mesh, PartitionSpec as P

EXPW = 2
CAP = 20
SB = 128
COL = ("y", "xh", "core")
BLK = ("zh", "zl", "xl")
SIZES = {"y": 4, "xh": 2, "core": 2, "zh": 8, "zl": 2, "xl": 2}
ZH = SIZES["zh"]
NEAR = SIZES["zl"] * SIZES["xl"]
GROUP = SIZES["y"] * SIZES["xh"]
F32 = jnp.float32
BF16 = jnp.bfloat16
SHIFT = 64.0


def dispatch(route_ids, route_gates):
    expert_ids = jnp.arange(EXPW, dtype=jnp.int32)
    matches = route_ids[:, :, None] == expert_ids[None, None, :]
    chosen = jnp.any(matches, axis=1)
    combine_weights = jnp.sum(
        jnp.where(matches, route_gates[:, :, None], jnp.zeros((), route_gates.dtype)), axis=1
    )
    slot_index = jnp.cumsum(chosen.astype(jnp.int32), axis=0) - 1
    onehot = chosen[:, :, None] & (
        slot_index[:, :, None] == jnp.arange(CAP, dtype=jnp.int32)[None, None, :]
    )
    return (onehot, combine_weights)


def swap(value):
    return lax.ppermute(value, "core", [(0, 1), (1, 0)])


def trade(value, axes):
    return lax.all_to_all(value, axes, 0, 0, tiled=True)


def gather(value, axes, count):
    return trade(jnp.broadcast_to(value[None], (count,) + value.shape), axes)


def pick(array, index):
    return lax.dynamic_index_in_dim(array, index, 0, keepdims=False)


def scale_row(read, blocks):
    return jnp.concatenate([jnp.full((1, SB), read(block), F32) for block in blocks], axis=1)


def gate_up_kernel(core_ref, gs_ref, us_ref, rs_ref, x_ref, gw_ref, uw_ref, rw_ref, o_ref):
    core = core_ref[0]
    depth, units = gw_ref.shape[1], gw_ref.shape[2]
    ks, ns = depth // SB, units // SB
    chunk = 2 * SB
    for which, (own_scale, own_weight) in enumerate(((gs_ref, gw_ref), (us_ref, uw_ref))):
        for n in range(units // chunk):
            columns = slice(n * chunk, (n + 1) * chunk)
            blocks = (2 * n, 2 * n + 1)
            total = None
            for other in (0, 1):
                base = (core if other == 0 else 1 - core) * depth
                for k in range(ks):
                    offset = pl.multiple_of(base + k * SB, SB)
                    rows = x_ref[0, :, pl.ds(offset, SB)]
                    if other == 0:
                        weight = own_weight[0, k * SB : (k + 1) * SB, columns]
                        row = scale_row(lambda c: own_scale[core, k, c] * SHIFT, blocks)
                    else:
                        first = which * depth + k * SB
                        weight = rw_ref[first : first + SB, columns]
                        place = (which * ks + k) * ns
                        row = scale_row(lambda c: rs_ref[0, place + c] * SHIFT, blocks)
                    product = jnp.dot(rows, weight, preferred_element_type=F32) * row
                    total = product if total is None else total + product
            left = which * units + n * chunk
            o_ref[:, :, left : left + chunk] = total.reshape(o_ref.shape[:2] + (chunk,))


def gate_up(core_index, portion, gate_weight, up_weight, other, gate_scale, up_scale, other_scale):
    near, near_rows, width2 = portion.shape
    _, depth, units = gate_weight.shape
    per = GROUP // near
    smem = pl.BlockSpec(memory_space=pltpu.SMEM)
    return pl.pallas_call(
        gate_up_kernel,
        grid_spec=pltpu.PrefetchScalarGridSpec(
            num_scalar_prefetch=1,
            grid=(near,),
            in_specs=[
                smem,
                smem,
                smem,
                pl.BlockSpec((1, near_rows, width2), lambda i, c: (i, 0, 0)),
                pl.BlockSpec((1, depth, units), lambda i, c: (c[0], 0, 0)),
                pl.BlockSpec((1, depth, units), lambda i, c: (c[0], 0, 0)),
                pl.BlockSpec((2 * depth, units), lambda i, c: (0, 0)),
            ],
            out_specs=pl.BlockSpec((per, near_rows // per, 2 * units), lambda i, c: (i, 0, 0)),
        ),
        out_shape=jax.ShapeDtypeStruct((GROUP, near_rows // per, 2 * units), F32),
        compiler_params=pltpu.CompilerParams(vmem_limit_bytes=24 * 1024 * 1024),
        cost_estimate=pl.CostEstimate(
            flops=2 * near * near_rows * width2 * 2 * units,
            bytes_accessed=near * near_rows * (2 * width2 + 8 * units) + 8 * depth * units,
            transcendentals=0,
        ),
        name="gate_up",
    )(core_index, gate_scale, up_scale, other_scale, portion, gate_weight, up_weight, other)


def down_kernel(core_ref, ds_ref, rs_ref, h_ref, dw_ref, rw_ref, o_ref):
    core = core_ref[0]
    depth, width = dw_ref.shape[1], dw_ref.shape[2]
    ks, ns = depth // SB, width // SB
    rows = h_ref.shape[0] * h_ref.shape[1]
    start = rs_ref.shape[1] - ks * ns
    for other in (0, 1):
        total = None
        for k in range(ks):
            cut = slice(k * SB, (k + 1) * SB)
            hidden = h_ref[:, :, cut].reshape(rows, SB)
            if other == 0:
                weight = dw_ref[0, cut, :]
                row = scale_row(lambda c: ds_ref[core, k, c], range(ns))
            else:
                weight = rw_ref[cut, :]
                row = scale_row(lambda c: rs_ref[0, start + k * ns + c], range(ns))
            product = jnp.dot(hidden, weight, preferred_element_type=F32) * row
            total = product if total is None else total + product
        base = pl.multiple_of((core if other == 0 else 1 - core) * width, SB)
        o_ref[0, :, pl.ds(base, width)] = total.astype(o_ref.dtype)


def down_project(core_index, hidden, down_weight, other, down_scale, other_scale):
    _, some_rows, depth = hidden.shape
    width = down_weight.shape[2]
    per = GROUP // NEAR
    smem = pl.BlockSpec(memory_space=pltpu.SMEM)
    return pl.pallas_call(
        down_kernel,
        grid_spec=pltpu.PrefetchScalarGridSpec(
            num_scalar_prefetch=1,
            grid=(NEAR,),
            in_specs=[
                smem,
                smem,
                pl.BlockSpec((per, some_rows, depth), lambda i, c: (i, 0, 0)),
                pl.BlockSpec((1, depth, width), lambda i, c: (c[0], 0, 0)),
                pl.BlockSpec((depth, width), lambda i, c: (0, 0)),
            ],
            out_specs=pl.BlockSpec((1, per * some_rows, 2 * width), lambda i, c: (i, 0, 0)),
        ),
        out_shape=jax.ShapeDtypeStruct((NEAR, per * some_rows, 2 * width), BF16),
        compiler_params=pltpu.CompilerParams(vmem_limit_bytes=24 * 1024 * 1024),
        cost_estimate=pl.CostEstimate(
            flops=4 * GROUP * some_rows * depth * width,
            bytes_accessed=GROUP * some_rows * (2 * depth + 4 * width) + 4 * depth * width,
            transcendentals=0,
        ),
        name="down_project",
    )(core_index, down_scale, other_scale, hidden, down_weight, other)


def shards(
    tokens,
    route_ids,
    route_gates,
    gate_weight,
    up_weight,
    gate_scale,
    up_scale,
    down_weight,
    down_scale,
):
    core = lax.axis_index("core")
    width = tokens.shape[1]
    hidden_width = gate_weight.shape[2]
    near_rows = ZH * CAP
    onehot, combine_weights = dispatch(route_ids, route_gates)
    slot_rows = jnp.einsum(
        "tec,td->ecd", onehot.astype(BF16), tokens, preferred_element_type=F32
    ).astype(BF16)
    packed = slot_rows.reshape(2, 4, CAP // 4 * width)
    far = jnp.broadcast_to(packed[None], (ZH,) + packed.shape).reshape(2 * ZH, 4, -1)
    far = trade(far, ("zh", "core")).reshape(ZH, 2, CAP, width)
    far = far.transpose(0, 2, 1, 3).reshape(near_rows, 2 * width)
    portion = gather(far, ("zl", "xl"), NEAR)

    other = 1 - core
    other_gate_up = swap(jnp.concatenate([pick(gate_weight, other), pick(up_weight, other)], axis=0))
    scales = [pick(scale, other).reshape(1, -1) for scale in (gate_scale, up_scale, down_scale)]
    other_scales = swap(jnp.concatenate(scales, axis=1))
    core_index = jnp.reshape(core, (1,)).astype(jnp.int32)

    partial_sums = gate_up(
        core_index,
        portion,
        gate_weight,
        up_weight,
        other_gate_up,
        gate_scale,
        up_scale,
        other_scales,
    ).astype(jnp.float16)
    received = trade(partial_sums, ("y", "xh"))
    summed = jnp.sum(received.astype(F32), axis=0) * (1.0 / SHIFT)
    hidden = (jax.nn.silu(summed[:, :hidden_width]) * summed[:, hidden_width:]).astype(BF16)
    hidden, other_down = lax.optimization_barrier((hidden, pick(down_weight, other)))
    other_down = swap(other_down)
    hidden = gather(hidden, ("y", "xh"), GROUP)
    down = down_project(core_index, hidden, down_weight, other_down, down_scale, other_scales)
    down = trade(down, ("zl", "xl"))
    down = jnp.sum(down.astype(F32), axis=0).astype(BF16)
    down = down.reshape(ZH, CAP, 2, width).transpose(0, 2, 1, 3).reshape(2 * ZH, 4, -1)
    down = trade(down, ("zh", "core")).reshape(ZH, 2, 4, -1)
    expert_out = jnp.sum(down.astype(F32), axis=0).reshape(2, CAP, width)

    combine = onehot.astype(F32) * combine_weights[:, :, None]
    mixed = jnp.einsum("tec,ecd->td", combine, expert_out, precision=lax.Precision.HIGHEST)
    return mixed.astype(BF16)


def solution(mesh):
    parts = Mesh(mesh.devices.reshape(tuple(SIZES.values())), tuple(SIZES))
    in_specs = (
        P(BLK, COL),
        P(BLK, None),
        P(BLK, None),
        P(None, COL, BLK),
        P(None, COL, BLK),
        P(None, COL, BLK),
        P(None, COL, BLK),
        P(None, BLK, COL),
        P(None, BLK, COL),
    )
    return jax.shard_map(
        shards, mesh=parts, in_specs=in_specs, out_specs=P(BLK, COL), check_vma=False
    )
```

```python
import jax
import jax.numpy as jnp
from jax import lax
from jax.experimental import pallas as pl
from jax.experimental.pallas import tpu as pltpu
from jax.sharding import Mesh, PartitionSpec as P

EXPW = 2
CAP = 20
SB = 128
COL = ("y", "xh", "core")
BLK = ("zh", "zl", "xl")
SIZES = {"y": 4, "xh": 2, "core": 2, "zh": 8, "zl": 2, "xl": 2}
ZH = SIZES["zh"]
NEAR = SIZES["zl"] * SIZES["xl"]
GROUP = SIZES["y"] * SIZES["xh"]
F32 = jnp.float32
BF16 = jnp.bfloat16
SHIFT = 64.0


def dispatch(route_ids, route_gates):
    expert_ids = jnp.arange(EXPW, dtype=jnp.int32)
    matches = route_ids[:, :, None] == expert_ids[None, None, :]
    chosen = jnp.any(matches, axis=1)
    combine_weights = jnp.sum(
        jnp.where(matches, route_gates[:, :, None], jnp.zeros((), route_gates.dtype)), axis=1
    )
    slot_index = jnp.cumsum(chosen.astype(jnp.int32), axis=0) - 1
    onehot = chosen[:, :, None] & (
        slot_index[:, :, None] == jnp.arange(CAP, dtype=jnp.int32)[None, None, :]
    )
    return (onehot, combine_weights)


def swap(value):
    return lax.ppermute(value, "core", [(0, 1), (1, 0)])


def trade(value, axes):
    return lax.all_to_all(value, axes, 0, 0, tiled=True)


def gather(value, axes, count):
    return trade(jnp.broadcast_to(value[None], (count,) + value.shape), axes)


def pick(array, index):
    return lax.dynamic_index_in_dim(array, index, 0, keepdims=False)


def flat_scales(scales, expert):
    return jnp.concatenate([pick(scale, expert).reshape(1, -1) for scale in scales], axis=1)


def scale_row(read, blocks):
    return jnp.concatenate([jnp.full((1, SB), read(block), F32) for block in blocks], axis=1)


def gate_up_kernel(core_ref, os_ref, rs_ref, x_ref, gw_ref, uw_ref, rw_ref, o_ref):
    core = core_ref[0]
    depth, units = gw_ref.shape[1], gw_ref.shape[2]
    ks, ns = depth // SB, units // SB
    chunk = 2 * SB
    for which, own_weight in enumerate((gw_ref, uw_ref)):
        for n in range(units // chunk):
            columns = slice(n * chunk, (n + 1) * chunk)
            blocks = (2 * n, 2 * n + 1)
            total = None
            for other in (0, 1):
                base = (core if other == 0 else 1 - core) * depth
                for k in range(ks):
                    offset = pl.multiple_of(base + k * SB, SB)
                    rows = x_ref[0, :, pl.ds(offset, SB)]
                    place = (which * ks + k) * ns
                    if other == 0:
                        weight = own_weight[0, k * SB : (k + 1) * SB, columns]
                        row = scale_row(lambda c: os_ref[0, place + c] * SHIFT, blocks)
                    else:
                        first = which * depth + k * SB
                        weight = rw_ref[first : first + SB, columns]
                        row = scale_row(lambda c: rs_ref[0, place + c] * SHIFT, blocks)
                    product = jnp.dot(rows, weight, preferred_element_type=F32) * row
                    total = product if total is None else total + product
            left = which * units + n * chunk
            o_ref[:, :, left : left + chunk] = total.reshape(o_ref.shape[:2] + (chunk,))


def gate_up(core_index, portion, gate_weight, up_weight, other, own_scales, other_scales):
    near, near_rows, width2 = portion.shape
    _, depth, units = gate_weight.shape
    per = GROUP // near
    smem = pl.BlockSpec(memory_space=pltpu.SMEM)
    return pl.pallas_call(
        gate_up_kernel,
        grid_spec=pltpu.PrefetchScalarGridSpec(
            num_scalar_prefetch=1,
            grid=(near,),
            in_specs=[
                smem,
                smem,
                pl.BlockSpec((1, near_rows, width2), lambda i, c: (i, 0, 0)),
                pl.BlockSpec((1, depth, units), lambda i, c: (c[0], 0, 0)),
                pl.BlockSpec((1, depth, units), lambda i, c: (c[0], 0, 0)),
                pl.BlockSpec((2 * depth, units), lambda i, c: (0, 0)),
            ],
            out_specs=pl.BlockSpec((per, near_rows // per, 2 * units), lambda i, c: (i, 0, 0)),
        ),
        out_shape=jax.ShapeDtypeStruct((GROUP, near_rows // per, 2 * units), F32),
        compiler_params=pltpu.CompilerParams(vmem_limit_bytes=24 * 1024 * 1024),
        cost_estimate=pl.CostEstimate(
            flops=2 * near * near_rows * width2 * 2 * units,
            bytes_accessed=near * near_rows * (2 * width2 + 8 * units) + 8 * depth * units,
            transcendentals=0,
        ),
        name="gate_up",
    )(core_index, own_scales, other_scales, portion, gate_weight, up_weight, other)


def down_kernel(core_ref, os_ref, rs_ref, h_ref, dw_ref, rw_ref, o_ref):
    core = core_ref[0]
    depth, width = dw_ref.shape[1], dw_ref.shape[2]
    ks, ns = depth // SB, width // SB
    rows = h_ref.shape[0] * h_ref.shape[1]
    start = rs_ref.shape[1] - ks * ns
    for other in (0, 1):
        total = None
        for k in range(ks):
            cut = slice(k * SB, (k + 1) * SB)
            hidden = h_ref[:, :, cut].reshape(rows, SB)
            if other == 0:
                weight = dw_ref[0, cut, :]
                row = scale_row(lambda c: os_ref[0, start + k * ns + c], range(ns))
            else:
                weight = rw_ref[cut, :]
                row = scale_row(lambda c: rs_ref[0, start + k * ns + c], range(ns))
            product = jnp.dot(hidden, weight, preferred_element_type=F32) * row
            total = product if total is None else total + product
        base = pl.multiple_of((core if other == 0 else 1 - core) * width, SB)
        o_ref[0, :, pl.ds(base, width)] = total.astype(o_ref.dtype)


def down_project(core_index, hidden, down_weight, other, own_scales, other_scales):
    _, some_rows, depth = hidden.shape
    width = down_weight.shape[2]
    per = GROUP // NEAR
    smem = pl.BlockSpec(memory_space=pltpu.SMEM)
    return pl.pallas_call(
        down_kernel,
        grid_spec=pltpu.PrefetchScalarGridSpec(
            num_scalar_prefetch=1,
            grid=(NEAR,),
            in_specs=[
                smem,
                smem,
                pl.BlockSpec((per, some_rows, depth), lambda i, c: (i, 0, 0)),
                pl.BlockSpec((1, depth, width), lambda i, c: (c[0], 0, 0)),
                pl.BlockSpec((depth, width), lambda i, c: (0, 0)),
            ],
            out_specs=pl.BlockSpec((1, per * some_rows, 2 * width), lambda i, c: (i, 0, 0)),
        ),
        out_shape=jax.ShapeDtypeStruct((NEAR, per * some_rows, 2 * width), BF16),
        compiler_params=pltpu.CompilerParams(vmem_limit_bytes=24 * 1024 * 1024),
        cost_estimate=pl.CostEstimate(
            flops=4 * GROUP * some_rows * depth * width,
            bytes_accessed=GROUP * some_rows * (2 * depth + 4 * width) + 4 * depth * width,
            transcendentals=0,
        ),
        name="down_project",
    )(core_index, own_scales, other_scales, hidden, down_weight, other)


def shards(
    tokens,
    route_ids,
    route_gates,
    gate_weight,
    up_weight,
    gate_scale,
    up_scale,
    down_weight,
    down_scale,
):
    core = lax.axis_index("core")
    width = tokens.shape[1]
    hidden_width = gate_weight.shape[2]
    near_rows = ZH * CAP
    onehot, combine_weights = dispatch(route_ids, route_gates)
    slot_rows = jnp.einsum(
        "tec,td->ecd", onehot.astype(BF16), tokens, preferred_element_type=F32
    ).astype(BF16)
    packed = slot_rows.reshape(2, 4, CAP // 4 * width)
    far = jnp.broadcast_to(packed[None], (ZH,) + packed.shape).reshape(2 * ZH, 4, -1)
    far = trade(far, ("zh", "core")).reshape(ZH, 2, CAP, width)
    far = far.transpose(0, 2, 1, 3).reshape(near_rows, 2 * width)
    other = 1 - core
    core_index = jnp.reshape(core, (1,)).astype(jnp.int32)
    scales = (gate_scale, up_scale, down_scale)
    own_scales = flat_scales(scales, core)
    other_scales = swap(flat_scales(scales, other))
    other_gate_up = swap(jnp.concatenate([pick(gate_weight, other), pick(up_weight, other)], axis=0))
    other_down = swap(pick(down_weight, other))
    combine = onehot.astype(F32) * combine_weights[:, :, None]
    (
        far,
        core_index,
        own_scales,
        other_scales,
        other_gate_up,
        other_down,
        combine,
    ) = lax.optimization_barrier(
        (far, core_index, own_scales, other_scales, other_gate_up, other_down, combine)
    )
    portion = gather(far, ("zl", "xl"), NEAR)

    partial_sums = gate_up(
        core_index, portion, gate_weight, up_weight, other_gate_up, own_scales, other_scales
    ).astype(jnp.float16)
    received = trade(partial_sums, ("y", "xh"))
    summed = jnp.sum(received.astype(F32), axis=0) * (1.0 / SHIFT)
    hidden = (jax.nn.silu(summed[:, :hidden_width]) * summed[:, hidden_width:]).astype(BF16)
    hidden = gather(hidden, ("y", "xh"), GROUP)
    down = down_project(core_index, hidden, down_weight, other_down, own_scales, other_scales)
    down = trade(down, ("zl", "xl"))
    down = jnp.sum(down.astype(F32), axis=0).astype(BF16)
    down = down.reshape(ZH, CAP, 2, width).transpose(0, 2, 1, 3).reshape(2 * ZH, 4, -1)
    down = trade(down, ("zh", "core")).reshape(ZH, 2, 4, -1)
    expert_out = jnp.sum(down.astype(F32), axis=0).reshape(2, CAP, width)

    mixed = jnp.einsum("tec,ecd->td", combine, expert_out, precision=lax.Precision.HIGHEST)
    return mixed.astype(BF16)


def solution(mesh):
    parts = Mesh(mesh.devices.reshape(tuple(SIZES.values())), tuple(SIZES))
    in_specs = (
        P(BLK, COL),
        P(BLK, None),
        P(BLK, None),
        P(None, COL, BLK),
        P(None, COL, BLK),
        P(None, COL, BLK),
        P(None, COL, BLK),
        P(None, BLK, COL),
        P(None, BLK, COL),
    )
    return jax.shard_map(
        shards, mesh=parts, in_specs=in_specs, out_specs=P(BLK, COL), check_vma=False
    )
```

```python
import jax
import jax.numpy as jnp
from jax import lax
from jax.experimental import pallas as pl
from jax.experimental.pallas import tpu as pltpu
from jax.sharding import Mesh, PartitionSpec as P

EXPW = 2
CAP = 20
SB = 128
COL = ("y", "xh", "core")
BLK = ("zh", "zl", "xl")
SIZES = {"y": 4, "xh": 2, "core": 2, "zh": 8, "zl": 2, "xl": 2}
ZH = SIZES["zh"]
NEAR = SIZES["zl"] * SIZES["xl"]
GROUP = SIZES["y"] * SIZES["xh"]
F32 = jnp.float32
BF16 = jnp.bfloat16
SHIFT = 64.0


def dispatch(route_ids, route_gates):
    expert_ids = jnp.arange(EXPW, dtype=jnp.int32)
    matches = route_ids[:, :, None] == expert_ids[None, None, :]
    chosen = jnp.any(matches, axis=1)
    combine_weights = jnp.sum(
        jnp.where(matches, route_gates[:, :, None], jnp.zeros((), route_gates.dtype)), axis=1
    )
    slot_index = jnp.cumsum(chosen.astype(jnp.int32), axis=0) - 1
    onehot = chosen[:, :, None] & (
        slot_index[:, :, None] == jnp.arange(CAP, dtype=jnp.int32)[None, None, :]
    )
    return (onehot, combine_weights)


def swap(value):
    return lax.ppermute(value, "core", [(0, 1), (1, 0)])


def trade(value, axes):
    return lax.all_to_all(value, axes, 0, 0, tiled=True)


def gather(value, axes, count):
    return trade(jnp.broadcast_to(value[None], (count,) + value.shape), axes)


def pick(array, index):
    return lax.dynamic_index_in_dim(array, index, 0, keepdims=False)


def flat_scales(scales, expert):
    return jnp.concatenate([pick(scale, expert).reshape(1, -1) for scale in scales], axis=1)


def scale_row(read, blocks):
    return jnp.concatenate([jnp.full((1, SB), read(block), F32) for block in blocks], axis=1)


def gate_up_kernel(core_ref, os_ref, rs_ref, x_ref, gw_ref, uw_ref, rw_ref, o_ref):
    core = core_ref[0]
    near, _, _, depth = x_ref.shape
    units = gw_ref.shape[2]
    ks, ns = depth // SB, units // SB
    chunk = 2 * SB
    per = o_ref.shape[0] // near
    for i in range(near):
        for which, own_weight in enumerate((gw_ref, uw_ref)):
            for n in range(units // chunk):
                columns = slice(n * chunk, (n + 1) * chunk)
                blocks = (2 * n, 2 * n + 1)
                total = None
                for part, scale_ref in ((core, os_ref), (1 - core, rs_ref)):
                    for k in range(ks):
                        cut = slice(k * SB, (k + 1) * SB)
                        rows = x_ref[i, part, :, cut]
                        if scale_ref is os_ref:
                            weight = own_weight[0, cut, columns]
                        else:
                            first = which * depth + k * SB
                            weight = rw_ref[first : first + SB, columns]
                        place = (which * ks + k) * ns
                        row = scale_row(lambda c: scale_ref[0, place + c] * SHIFT, blocks)
                        product = jnp.dot(rows, weight, preferred_element_type=F32) * row
                        total = product if total is None else total + product
                left = which * units + n * chunk
                o_ref[i * per : (i + 1) * per, :, left : left + chunk] = total.reshape(
                    (per, o_ref.shape[1], chunk)
                )


def whole(shape):
    return pl.BlockSpec(shape, lambda i, c: (0,) * len(shape))


def expert_part(shape):
    return pl.BlockSpec((1,) + shape[1:], lambda i, c: (c[0],) + (0,) * (len(shape) - 1))


def gate_up(core_index, portion, gate_weight, up_weight, other, own_scales, other_scales):
    near, _, near_rows, depth = portion.shape
    units = gate_weight.shape[2]
    out = (GROUP, near * near_rows // GROUP, 2 * units)
    smem = pl.BlockSpec(memory_space=pltpu.SMEM)
    return pl.pallas_call(
        gate_up_kernel,
        grid_spec=pltpu.PrefetchScalarGridSpec(
            num_scalar_prefetch=1,
            grid=(1,),
            in_specs=[
                smem,
                smem,
                whole(portion.shape),
                expert_part(gate_weight.shape),
                expert_part(up_weight.shape),
                whole(other.shape),
            ],
            out_specs=whole(out),
        ),
        out_shape=jax.ShapeDtypeStruct(out, F32),
        compiler_params=pltpu.CompilerParams(vmem_limit_bytes=32 * 1024 * 1024),
        cost_estimate=pl.CostEstimate(
            flops=8 * near * near_rows * depth * units,
            bytes_accessed=near * near_rows * (4 * depth + 8 * units) + 8 * depth * units,
            transcendentals=0,
        ),
        name="gate_up",
    )(core_index, own_scales, other_scales, portion, gate_weight, up_weight, other)


def down_kernel(core_ref, os_ref, rs_ref, h_ref, dw_ref, rw_ref, o_ref):
    core = core_ref[0]
    near, _, rows, width = o_ref.shape
    depth = h_ref.shape[2]
    ks, ns = depth // SB, width // SB
    start = rs_ref.shape[1] - ks * ns
    per = h_ref.shape[0] // near
    for i in range(near):
        for part, scale_ref in ((core, os_ref), (1 - core, rs_ref)):
            total = None
            for k in range(ks):
                cut = slice(k * SB, (k + 1) * SB)
                hidden = h_ref[i * per : (i + 1) * per, :, cut].reshape(rows, SB)
                weight = dw_ref[0, cut, :] if scale_ref is os_ref else rw_ref[cut, :]
                row = scale_row(lambda c: scale_ref[0, start + k * ns + c], range(ns))
                product = jnp.dot(hidden, weight, preferred_element_type=F32) * row
                total = product if total is None else total + product
            o_ref[i, part] = total.astype(o_ref.dtype)


def down_project(core_index, hidden, down_weight, other, own_scales, other_scales):
    _, some_rows, depth = hidden.shape
    width = down_weight.shape[2]
    rows = GROUP * some_rows
    out = (NEAR, 2, rows // NEAR, width)
    smem = pl.BlockSpec(memory_space=pltpu.SMEM)
    return pl.pallas_call(
        down_kernel,
        grid_spec=pltpu.PrefetchScalarGridSpec(
            num_scalar_prefetch=1,
            grid=(1,),
            in_specs=[
                smem,
                smem,
                whole(hidden.shape),
                expert_part(down_weight.shape),
                whole(other.shape),
            ],
            out_specs=whole(out),
        ),
        out_shape=jax.ShapeDtypeStruct(out, BF16),
        compiler_params=pltpu.CompilerParams(vmem_limit_bytes=32 * 1024 * 1024),
        cost_estimate=pl.CostEstimate(
            flops=4 * rows * depth * width,
            bytes_accessed=rows * (2 * depth + 4 * width) + 4 * depth * width,
            transcendentals=0,
        ),
        name="down_project",
    )(core_index, own_scales, other_scales, hidden, down_weight, other)


def shards(
    tokens,
    route_ids,
    route_gates,
    gate_weight,
    up_weight,
    gate_scale,
    up_scale,
    down_weight,
    down_scale,
):
    core = lax.axis_index("core")
    width = tokens.shape[1]
    hidden_width = gate_weight.shape[2]
    near_rows = ZH * CAP
    onehot, combine_weights = dispatch(route_ids, route_gates)
    slot_rows = jnp.einsum(
        "tec,td->ecd", onehot.astype(BF16), tokens, preferred_element_type=F32
    ).astype(BF16)
    packed = slot_rows.reshape(8, -1)
    far = gather(packed, "zh", ZH).reshape(ZH, 2, CAP, width)
    far = far.transpose(1, 0, 2, 3).reshape(2, near_rows, width)

    other = 1 - core
    core_index = jnp.reshape(core, (1,)).astype(jnp.int32)
    scales = (gate_scale, up_scale, down_scale)
    own_scales = flat_scales(scales, core)
    other_scales = swap(flat_scales(scales, other))
    other_gate_up = swap(jnp.concatenate([pick(gate_weight, other), pick(up_weight, other)], axis=0))
    other_down = swap(pick(down_weight, other))
    combine = onehot.astype(F32) * combine_weights[:, :, None]
    (
        far,
        core_index,
        own_scales,
        other_scales,
        other_gate_up,
        other_down,
        combine,
    ) = lax.optimization_barrier(
        (far, core_index, own_scales, other_scales, other_gate_up, other_down, combine)
    )
    portion = jnp.broadcast_to(far[None], (NEAR,) + far.shape).reshape(2 * NEAR, near_rows, width)
    portion = trade(portion, ("zl", "xl", "core")).reshape(NEAR, 2, near_rows, width)

    partial_sums = gate_up(
        core_index, portion, gate_weight, up_weight, other_gate_up, own_scales, other_scales
    ).astype(jnp.float16)
    received = trade(partial_sums, ("y", "xh"))
    summed = jnp.sum(received.astype(F32), axis=0) * (1.0 / SHIFT)
    hidden = (jax.nn.silu(summed[:, :hidden_width]) * summed[:, hidden_width:]).astype(BF16)
    hidden = gather(hidden, ("y", "xh"), GROUP)
    down = down_project(core_index, hidden, down_weight, other_down, own_scales, other_scales)
    down = trade(down.reshape(2 * NEAR, near_rows, width), ("zl", "xl", "core"))
    down = jnp.sum(down.reshape(NEAR, 2, near_rows, width).astype(F32), axis=0).astype(BF16)
    down = down.reshape(2, ZH, CAP, width).transpose(1, 0, 2, 3).reshape(ZH, 8, -1)
    down = trade(down, "zh")
    expert_out = jnp.sum(down.astype(F32), axis=0).reshape(2, CAP, width)

    mixed = jnp.einsum("tec,ecd->td", combine, expert_out, precision=lax.Precision.HIGHEST)
    return mixed.astype(BF16)


def solution(mesh):
    parts = Mesh(mesh.devices.reshape(tuple(SIZES.values())), tuple(SIZES))
    in_specs = (
        P(BLK, COL),
        P(BLK, None),
        P(BLK, None),
        P(None, COL, BLK),
        P(None, COL, BLK),
        P(None, COL, BLK),
        P(None, COL, BLK),
        P(None, BLK, COL),
        P(None, BLK, COL),
    )
    return jax.shard_map(
        shards, mesh=parts, in_specs=in_specs, out_specs=P(BLK, COL), check_vma=False
    )
```

```python
import jax
import jax.numpy as jnp
from jax import lax
from jax.experimental import pallas as pl
from jax.experimental.pallas import tpu as pltpu
from jax.sharding import Mesh, PartitionSpec as P

EXPW = 2
CAP = 20
SB = 128
COL = ("y", "xh", "core")
BLK = ("zh", "zl", "xl")
SIZES = {"y": 4, "xh": 2, "core": 2, "zh": 8, "zl": 2, "xl": 2}
ZH = SIZES["zh"]
NEAR = SIZES["zl"] * SIZES["xl"]
GROUP = SIZES["y"] * SIZES["xh"]
F32 = jnp.float32
BF16 = jnp.bfloat16
SHIFT = 64.0


def dispatch(route_ids, route_gates):
    expert_ids = jnp.arange(EXPW, dtype=jnp.int32)
    matches = route_ids[:, :, None] == expert_ids[None, None, :]
    chosen = jnp.any(matches, axis=1)
    combine_weights = jnp.sum(
        jnp.where(matches, route_gates[:, :, None], jnp.zeros((), route_gates.dtype)), axis=1
    )
    slot_index = jnp.cumsum(chosen.astype(jnp.int32), axis=0) - 1
    onehot = chosen[:, :, None] & (
        slot_index[:, :, None] == jnp.arange(CAP, dtype=jnp.int32)[None, None, :]
    )
    return (onehot, combine_weights)


def swap(value):
    return lax.ppermute(value, "core", [(0, 1), (1, 0)])


def trade(value, axes):
    return lax.all_to_all(value, axes, 0, 0, tiled=True)


def gather(value, axes, count):
    return trade(jnp.broadcast_to(value[None], (count,) + value.shape), axes)


def pick(array, index):
    return lax.dynamic_index_in_dim(array, index, 0, keepdims=False)


def flat_scales(scales, expert):
    return jnp.concatenate([pick(scale, expert).reshape(1, -1) for scale in scales], axis=1)


def scale_row(read, blocks):
    return jnp.concatenate([jnp.full((1, SB), read(block), F32) for block in blocks], axis=1)


def gate_up_kernel(core_ref, os_ref, rs_ref, x_ref, gw_ref, uw_ref, rw_ref, o_ref):
    core = core_ref[0]
    near = x_ref.shape[0]
    depth, units = gw_ref.shape[1:]
    ks, ns = depth // SB, units // SB
    chunk = 2 * SB
    per = o_ref.shape[0] // near
    for i in range(near):
        for which, own_weight in enumerate((gw_ref, uw_ref)):
            for n in range(units // chunk):
                columns = slice(n * chunk, (n + 1) * chunk)
                blocks = (2 * n, 2 * n + 1)
                total = None
                for part, scale_ref in ((core, os_ref), (1 - core, rs_ref)):
                    for k in range(ks):
                        cut = slice(k * SB, (k + 1) * SB)
                        rows = x_ref[i, :, pl.ds(pl.multiple_of(part * depth + k * SB, SB), SB)]
                        if scale_ref is os_ref:
                            weight = own_weight[0, cut, columns]
                        else:
                            first = which * depth + k * SB
                            weight = rw_ref[first : first + SB, columns]
                        place = (which * ks + k) * ns
                        row = scale_row(lambda c: scale_ref[0, place + c] * SHIFT, blocks)
                        product = jnp.dot(rows, weight, preferred_element_type=F32) * row
                        total = product if total is None else total + product
                left = which * units + n * chunk
                o_ref[i * per : (i + 1) * per, :, left : left + chunk] = total.reshape(
                    (per, o_ref.shape[1], chunk)
                )


def whole(shape):
    return pl.BlockSpec(shape, lambda i, c: (0,) * len(shape))


def expert_part(shape):
    return pl.BlockSpec((1,) + shape[1:], lambda i, c: (c[0],) + (0,) * (len(shape) - 1))


def gate_up(core_index, portion, gate_weight, up_weight, other, own_scales, other_scales):
    near, near_rows, _ = portion.shape
    depth, units = gate_weight.shape[1:]
    out = (GROUP, near * near_rows // GROUP, 2 * units)
    smem = pl.BlockSpec(memory_space=pltpu.SMEM)
    return pl.pallas_call(
        gate_up_kernel,
        grid_spec=pltpu.PrefetchScalarGridSpec(
            num_scalar_prefetch=1,
            grid=(1,),
            in_specs=[
                smem,
                smem,
                whole(portion.shape),
                expert_part(gate_weight.shape),
                expert_part(up_weight.shape),
                whole(other.shape),
            ],
            out_specs=whole(out),
        ),
        out_shape=jax.ShapeDtypeStruct(out, F32),
        compiler_params=pltpu.CompilerParams(vmem_limit_bytes=32 * 1024 * 1024),
        cost_estimate=pl.CostEstimate(
            flops=8 * near * near_rows * depth * units,
            bytes_accessed=near * near_rows * (4 * depth + 8 * units) + 8 * depth * units,
            transcendentals=0,
        ),
        name="gate_up",
    )(core_index, own_scales, other_scales, portion, gate_weight, up_weight, other)


def down_kernel(core_ref, os_ref, rs_ref, h_ref, dw_ref, rw_ref, o_ref):
    core = core_ref[0]
    near, rows, _ = o_ref.shape
    depth, width = rw_ref.shape
    ks, ns = depth // SB, width // SB
    start = rs_ref.shape[1] - ks * ns
    per = h_ref.shape[0] // near
    for i in range(near):
        for part, scale_ref in ((core, os_ref), (1 - core, rs_ref)):
            total = None
            for k in range(ks):
                cut = slice(k * SB, (k + 1) * SB)
                hidden = h_ref[i * per : (i + 1) * per, :, cut].reshape(rows, SB)
                weight = dw_ref[0, cut, :] if scale_ref is os_ref else rw_ref[cut, :]
                row = scale_row(lambda c: scale_ref[0, start + k * ns + c], range(ns))
                product = jnp.dot(hidden, weight, preferred_element_type=F32) * row
                total = product if total is None else total + product
            o_ref[i, :, pl.ds(pl.multiple_of(part * width, SB), width)] = total.astype(o_ref.dtype)


def down_project(core_index, hidden, down_weight, other, own_scales, other_scales):
    _, some_rows, depth = hidden.shape
    width = down_weight.shape[2]
    rows = GROUP * some_rows
    out = (NEAR, rows // NEAR, 2 * width)
    smem = pl.BlockSpec(memory_space=pltpu.SMEM)
    return pl.pallas_call(
        down_kernel,
        grid_spec=pltpu.PrefetchScalarGridSpec(
            num_scalar_prefetch=1,
            grid=(1,),
            in_specs=[
                smem,
                smem,
                whole(hidden.shape),
                expert_part(down_weight.shape),
                whole(other.shape),
            ],
            out_specs=whole(out),
        ),
        out_shape=jax.ShapeDtypeStruct(out, BF16),
        compiler_params=pltpu.CompilerParams(vmem_limit_bytes=32 * 1024 * 1024),
        cost_estimate=pl.CostEstimate(
            flops=4 * rows * depth * width,
            bytes_accessed=rows * (2 * depth + 4 * width) + 4 * depth * width,
            transcendentals=0,
        ),
        name="down_project",
    )(core_index, own_scales, other_scales, hidden, down_weight, other)


def shards(
    tokens,
    route_ids,
    route_gates,
    gate_weight,
    up_weight,
    gate_scale,
    up_scale,
    down_weight,
    down_scale,
):
    core = lax.axis_index("core")
    zero = core == 0
    width = tokens.shape[1]
    hidden_width = gate_weight.shape[2]
    near_rows = ZH * CAP
    other_tokens = swap(tokens)
    onehot, combine_weights = dispatch(route_ids, route_gates)
    own = jnp.where(zero, onehot[:, 0], onehot[:, 1]).astype(BF16)
    both = [jnp.where(zero, tokens, other_tokens), jnp.where(zero, other_tokens, tokens)]
    slot_rows = jnp.einsum(
        "tc,td->cd", own, jnp.concatenate(both, axis=1), preferred_element_type=F32
    ).astype(BF16)
    slot_rows, gate_weight, up_weight, down_weight, gate_scale, up_scale, down_scale = (
        lax.optimization_barrier(
            (slot_rows, gate_weight, up_weight, down_weight, gate_scale, up_scale, down_scale)
        )
    )
    far = gather(slot_rows.reshape(8, -1), "zh", ZH).reshape(near_rows, 2 * width)

    other = 1 - core
    core_index = jnp.reshape(core, (1,)).astype(jnp.int32)
    scales = (gate_scale, up_scale, down_scale)
    own_scales = flat_scales(scales, core)
    other_scales = swap(flat_scales(scales, other))
    other_gate_up = swap(jnp.concatenate([pick(gate_weight, other), pick(up_weight, other)], axis=0))
    other_down = swap(pick(down_weight, other))
    combine = onehot.astype(F32) * combine_weights[:, :, None]
    own_combine = jnp.where(zero, combine[:, 0], combine[:, 1])
    other_combine = jnp.where(zero, combine[:, 1], combine[:, 0])
    (
        far,
        zero,
        core_index,
        own_scales,
        other_scales,
        other_gate_up,
        other_down,
        own_combine,
        other_combine,
    ) = lax.optimization_barrier(
        (
            far,
            zero,
            core_index,
            own_scales,
            other_scales,
            other_gate_up,
            other_down,
            own_combine,
            other_combine,
        )
    )
    portion = gather(far, ("zl", "xl"), NEAR)

    partial_sums = gate_up(
        core_index, portion, gate_weight, up_weight, other_gate_up, own_scales, other_scales
    ).astype(jnp.float16)
    received = trade(partial_sums, ("y", "xh"))
    summed = jnp.sum(received.astype(F32), axis=0) * (1.0 / SHIFT)
    hidden = (jax.nn.silu(summed[:, :hidden_width]) * summed[:, hidden_width:]).astype(BF16)
    hidden = gather(hidden, ("y", "xh"), GROUP)
    down = down_project(core_index, hidden, down_weight, other_down, own_scales, other_scales)
    down = trade(down, ("zl", "xl"))
    down = jnp.sum(down.astype(F32), axis=0).astype(BF16)
    down = trade(down.reshape(ZH, 8, -1), "zh")
    out = jnp.sum(down.astype(F32), axis=0).reshape(CAP, 2 * width)
    first, second = out[:, :width], out[:, width:]
    given = swap(jnp.where(zero, second, first))
    mixed = jnp.dot(own_combine, jnp.where(zero, first, second), precision=lax.Precision.HIGHEST)
    mixed = mixed + jnp.dot(other_combine, given, precision=lax.Precision.HIGHEST)
    return mixed.astype(BF16)


def solution(mesh):
    parts = Mesh(mesh.devices.reshape(tuple(SIZES.values())), tuple(SIZES))
    in_specs = (
        P(BLK, COL),
        P(BLK, None),
        P(BLK, None),
        P(None, COL, BLK),
        P(None, COL, BLK),
        P(None, COL, BLK),
        P(None, COL, BLK),
        P(None, BLK, COL),
        P(None, BLK, COL),
    )
    return jax.shard_map(
        shards, mesh=parts, in_specs=in_specs, out_specs=P(BLK, COL), check_vma=False
    )
```

```python
import jax
import jax.numpy as jnp
from jax import lax
from jax.experimental import pallas as pl
from jax.experimental.pallas import tpu as pltpu
from jax.sharding import Mesh, PartitionSpec as P

EXPW = 2
CAP = 20
SB = 128
COL = ("y", "xh", "core")
BLK = ("zh", "zl", "xl")
SIZES = {"y": 4, "xh": 2, "core": 2, "zh": 8, "zl": 2, "xl": 2}
ZH = SIZES["zh"]
NEAR = SIZES["zl"] * SIZES["xl"]
GROUP = SIZES["y"] * SIZES["xh"]
F32 = jnp.float32
BF16 = jnp.bfloat16
SHIFT = 64.0


def matching(route_ids):
    expert_ids = jnp.arange(EXPW, dtype=jnp.int32)
    return route_ids[:, :, None] == expert_ids[None, None, :]


def dispatch(route_ids):
    chosen = jnp.any(matching(route_ids), axis=1)
    slot_index = jnp.cumsum(chosen.astype(jnp.int32), axis=0) - 1
    return chosen[:, :, None] & (
        slot_index[:, :, None] == jnp.arange(CAP, dtype=jnp.int32)[None, None, :]
    )


def combine_weights(route_ids, route_gates):
    return jnp.sum(
        jnp.where(
            matching(route_ids), route_gates[:, :, None], jnp.zeros((), route_gates.dtype)
        ),
        axis=1,
    )


def swap(value):
    return lax.ppermute(value, "core", [(0, 1), (1, 0)])


def trade(value, axes):
    return lax.all_to_all(value, axes, 0, 0, tiled=True)


def gather(value, axes, count):
    return trade(jnp.broadcast_to(value[None], (count,) + value.shape), axes)


def pick(array, index):
    return lax.dynamic_index_in_dim(array, index, 0, keepdims=False)


def flat_scales(scales, expert):
    return jnp.concatenate([pick(scale, expert).reshape(1, -1) for scale in scales], axis=1)


def scale_row(read, blocks):
    return jnp.concatenate([jnp.full((1, SB), read(block), F32) for block in blocks], axis=1)


def gate_up_kernel(core_ref, os_ref, rs_ref, x_ref, gw_ref, uw_ref, rw_ref, o_ref):
    near = x_ref.shape[0]
    depth, units = gw_ref.shape[1:]
    ks, ns = depth // SB, units // SB
    chunk = 2 * SB
    per = o_ref.shape[0] // near
    for i in range(near):
        for which, own_weight in enumerate((gw_ref, uw_ref)):
            for n in range(units // chunk):
                columns = slice(n * chunk, (n + 1) * chunk)
                blocks = (2 * n, 2 * n + 1)
                total = None
                for part, scale_ref in enumerate((os_ref, rs_ref)):
                    for k in range(ks):
                        cut = slice(k * SB, (k + 1) * SB)
                        start = part * depth + k * SB
                        rows = x_ref[i, :, start : start + SB]
                        if scale_ref is os_ref:
                            weight = own_weight[0, cut, columns]
                        else:
                            first = which * depth + k * SB
                            weight = rw_ref[first : first + SB, columns]
                        place = (which * ks + k) * ns
                        row = scale_row(lambda c: scale_ref[0, place + c] * SHIFT, blocks)
                        product = jnp.dot(rows, weight, preferred_element_type=F32) * row
                        total = product if total is None else total + product
                left = which * units + n * chunk
                o_ref[i * per : (i + 1) * per, :, left : left + chunk] = total.reshape(
                    (per, o_ref.shape[1], chunk)
                )


def whole(shape):
    return pl.BlockSpec(shape, lambda i, c: (0,) * len(shape))


def expert_part(shape):
    return pl.BlockSpec((1,) + shape[1:], lambda i, c: (c[0],) + (0,) * (len(shape) - 1))


def gate_up(core_index, portion, gate_weight, up_weight, other, own_scales, other_scales):
    near, near_rows, _ = portion.shape
    depth, units = gate_weight.shape[1:]
    out = (GROUP, near * near_rows // GROUP, 2 * units)
    smem = pl.BlockSpec(memory_space=pltpu.SMEM)
    return pl.pallas_call(
        gate_up_kernel,
        grid_spec=pltpu.PrefetchScalarGridSpec(
            num_scalar_prefetch=1,
            grid=(1,),
            in_specs=[
                smem,
                smem,
                whole(portion.shape),
                expert_part(gate_weight.shape),
                expert_part(up_weight.shape),
                whole(other.shape),
            ],
            out_specs=whole(out),
        ),
        out_shape=jax.ShapeDtypeStruct(out, F32),
        compiler_params=pltpu.CompilerParams(vmem_limit_bytes=32 * 1024 * 1024),
        cost_estimate=pl.CostEstimate(
            flops=8 * near * near_rows * depth * units,
            bytes_accessed=near * near_rows * (4 * depth + 8 * units) + 8 * depth * units,
            transcendentals=0,
        ),
        name="gate_up",
    )(core_index, own_scales, other_scales, portion, gate_weight, up_weight, other)


def down_kernel(core_ref, os_ref, rs_ref, h_ref, dw_ref, rw_ref, o_ref):
    near, rows, _ = o_ref.shape
    depth, width = rw_ref.shape
    ks, ns = depth // SB, width // SB
    start = rs_ref.shape[1] - ks * ns
    per = h_ref.shape[0] // near
    for i in range(near):
        for part, scale_ref in enumerate((os_ref, rs_ref)):
            total = None
            for k in range(ks):
                cut = slice(k * SB, (k + 1) * SB)
                hidden = h_ref[i * per : (i + 1) * per, :, cut].reshape(rows, SB)
                weight = dw_ref[0, cut, :] if scale_ref is os_ref else rw_ref[cut, :]
                row = scale_row(lambda c: scale_ref[0, start + k * ns + c], range(ns))
                product = jnp.dot(hidden, weight, preferred_element_type=F32) * row
                total = product if total is None else total + product
            o_ref[i, :, part * width : (part + 1) * width] = total.astype(o_ref.dtype)


def down_project(core_index, hidden, down_weight, other, own_scales, other_scales):
    _, some_rows, depth = hidden.shape
    width = down_weight.shape[2]
    rows = GROUP * some_rows
    out = (NEAR, rows // NEAR, 2 * width)
    smem = pl.BlockSpec(memory_space=pltpu.SMEM)
    return pl.pallas_call(
        down_kernel,
        grid_spec=pltpu.PrefetchScalarGridSpec(
            num_scalar_prefetch=1,
            grid=(1,),
            in_specs=[
                smem,
                smem,
                whole(hidden.shape),
                expert_part(down_weight.shape),
                whole(other.shape),
            ],
            out_specs=whole(out),
        ),
        out_shape=jax.ShapeDtypeStruct(out, BF16),
        compiler_params=pltpu.CompilerParams(vmem_limit_bytes=32 * 1024 * 1024),
        cost_estimate=pl.CostEstimate(
            flops=4 * rows * depth * width,
            bytes_accessed=rows * (2 * depth + 4 * width) + 4 * depth * width,
            transcendentals=0,
        ),
        name="down_project",
    )(core_index, own_scales, other_scales, hidden, down_weight, other)


def shards(
    tokens,
    route_ids,
    route_gates,
    gate_weight,
    up_weight,
    gate_scale,
    up_scale,
    down_weight,
    down_scale,
):
    core = lax.axis_index("core")
    zero = core == 0
    width = tokens.shape[1]
    hidden_width = gate_weight.shape[2]
    near_rows = ZH * CAP
    other_tokens = swap(tokens)
    onehot = dispatch(route_ids)
    own = jnp.where(zero, onehot[:, 0], onehot[:, 1]).astype(BF16)
    slot_rows = [
        jnp.einsum("tc,td->cd", own, part, preferred_element_type=F32).astype(BF16)
        for part in (tokens, other_tokens)
    ]
    slot_rows = jnp.concatenate(slot_rows, axis=1).reshape(8, -1)
    (
        slot_rows,
        onehot,
        route_ids,
        route_gates,
        gate_weight,
        up_weight,
        down_weight,
        gate_scale,
        up_scale,
        down_scale,
    ) = lax.optimization_barrier(
        (
            slot_rows,
            onehot,
            route_ids,
            route_gates,
            gate_weight,
            up_weight,
            down_weight,
            gate_scale,
            up_scale,
            down_scale,
        )
    )
    far = gather(slot_rows, "zh", ZH).reshape(near_rows, 2 * width)

    other = 1 - core
    core_index = jnp.reshape(core, (1,)).astype(jnp.int32)
    sent = jnp.concatenate([pick(gate_weight, other), pick(up_weight, other)], axis=0)
    sent_down, gate_scale, up_scale, down_scale = lax.optimization_barrier(
        (pick(down_weight, other), gate_scale, up_scale, down_scale)
    )
    scales = (gate_scale, up_scale, down_scale)
    own_scales = flat_scales(scales, core)
    other_scales = swap(flat_scales(scales, other))
    other_gate_up = swap(sent)
    other_down = swap(sent_down)
    combine = onehot.astype(F32) * combine_weights(route_ids, route_gates)[:, :, None]
    own_combine = jnp.where(zero, combine[:, 0], combine[:, 1])
    other_combine = jnp.where(zero, combine[:, 1], combine[:, 0])
    (
        far,
        core_index,
        own_scales,
        other_scales,
        other_gate_up,
        other_down,
        own_combine,
        other_combine,
    ) = lax.optimization_barrier(
        (
            far,
            core_index,
            own_scales,
            other_scales,
            other_gate_up,
            other_down,
            own_combine,
            other_combine,
        )
    )
    portion = gather(far, ("zl", "xl"), NEAR)

    partial_sums = gate_up(
        core_index, portion, gate_weight, up_weight, other_gate_up, own_scales, other_scales
    ).astype(jnp.float16)
    received = trade(partial_sums, ("y", "xh"))
    summed = jnp.sum(received.astype(F32), axis=0) * (1.0 / SHIFT)
    hidden = (jax.nn.silu(summed[:, :hidden_width]) * summed[:, hidden_width:]).astype(BF16)
    hidden = gather(hidden, ("y", "xh"), GROUP)
    down = down_project(core_index, hidden, down_weight, other_down, own_scales, other_scales)
    down = trade(down, ("zl", "xl"))
    down = jnp.sum(down.astype(F32), axis=0).astype(BF16)
    down = trade(down.reshape(ZH, 8, -1), "zh")
    out = jnp.sum(down.astype(F32), axis=0).reshape(CAP, 2 * width)
    given = swap(out[:, width:])
    mixed = jnp.dot(own_combine, out[:, :width], precision=lax.Precision.HIGHEST)
    mixed = mixed + jnp.dot(other_combine, given, precision=lax.Precision.HIGHEST)
    return mixed.astype(BF16)


def solution(mesh):
    parts = Mesh(mesh.devices.reshape(tuple(SIZES.values())), tuple(SIZES))
    in_specs = (
        P(BLK, COL),
        P(BLK, None),
        P(BLK, None),
        P(None, COL, BLK),
        P(None, COL, BLK),
        P(None, COL, BLK),
        P(None, COL, BLK),
        P(None, BLK, COL),
        P(None, BLK, COL),
    )
    return jax.shard_map(
        shards, mesh=parts, in_specs=in_specs, out_specs=P(BLK, COL), check_vma=False
    )
```

```python
import jax
import jax.numpy as jnp
from jax import lax
from jax.experimental import pallas as pl
from jax.experimental.pallas import tpu as pltpu
from jax.sharding import Mesh, PartitionSpec as P

EXPW = 2
CAP = 20
SB = 128
COL = ("ya", "yb", "xh", "core")
BLK = ("za", "zb", "zc", "zl", "xl")
FAR = ("zc", "zb", "za")
NEIGHBOURS = ("xl", "zl")
PLANE = ("ya", "yb", "xh")
SIZES = dict.fromkeys(COL + BLK, 2)
ZH = 2 ** len(FAR)
NEAR = 2 ** len(NEIGHBOURS)
GROUP = 2 ** len(PLANE)
F32 = jnp.float32
BF16 = jnp.bfloat16
SHIFT = 64.0


def matching(route_ids):
    expert_ids = jnp.arange(EXPW, dtype=jnp.int32)
    return route_ids[:, :, None] == expert_ids[None, None, :]


def dispatch(route_ids):
    chosen = jnp.any(matching(route_ids), axis=1)
    slot_index = jnp.cumsum(chosen.astype(jnp.int32), axis=0) - 1
    return chosen[:, :, None] & (
        slot_index[:, :, None] == jnp.arange(CAP, dtype=jnp.int32)[None, None, :]
    )


def combine_weights(route_ids, route_gates):
    return jnp.sum(
        jnp.where(
            matching(route_ids), route_gates[:, :, None], jnp.zeros((), route_gates.dtype)
        ),
        axis=1,
    )


def swap(value):
    return lax.ppermute(value, "core", [(0, 1), (1, 0)])


def trade(value, axes):
    return lax.all_to_all(value, axes, 0, 0, tiled=True)


def gather(value, axes, count):
    return trade(jnp.broadcast_to(value[None], (count,) + value.shape), axes)


def pick(array, index):
    return lax.dynamic_index_in_dim(array, index, 0, keepdims=False)


def flat_scales(scales, expert):
    return jnp.concatenate([pick(scale, expert).reshape(1, -1) for scale in scales], axis=1)


def scale_row(read, blocks):
    return jnp.concatenate([jnp.full((1, SB), read(block), F32) for block in blocks], axis=1)


def gate_up_kernel(core_ref, os_ref, rs_ref, x_ref, gw_ref, uw_ref, rw_ref, o_ref):
    near = x_ref.shape[0]
    depth, units = gw_ref.shape[1:]
    ks, ns = depth // SB, units // SB
    chunk = 2 * SB
    per = o_ref.shape[0] // near
    for i in range(near):
        for which, own_weight in enumerate((gw_ref, uw_ref)):
            for n in range(units // chunk):
                columns = slice(n * chunk, (n + 1) * chunk)
                blocks = (2 * n, 2 * n + 1)
                total = None
                for part, scale_ref in enumerate((os_ref, rs_ref)):
                    for k in range(ks):
                        cut = slice(k * SB, (k + 1) * SB)
                        start = part * depth + k * SB
                        rows = x_ref[i, :, start : start + SB]
                        if scale_ref is os_ref:
                            weight = own_weight[0, cut, columns]
                        else:
                            first = which * depth + k * SB
                            weight = rw_ref[first : first + SB, columns]
                        place = (which * ks + k) * ns
                        row = scale_row(lambda c: scale_ref[0, place + c] * SHIFT, blocks)
                        product = jnp.dot(rows, weight, preferred_element_type=F32) * row
                        total = product if total is None else total + product
                left = which * units + n * chunk
                o_ref[i * per : (i + 1) * per, :, left : left + chunk] = total.reshape(
                    (per, o_ref.shape[1], chunk)
                )


def whole(shape):
    return pl.BlockSpec(shape, lambda i, c: (0,) * len(shape))


def expert_part(shape):
    return pl.BlockSpec((1,) + shape[1:], lambda i, c: (c[0],) + (0,) * (len(shape) - 1))


def gate_up(core_index, portion, gate_weight, up_weight, other, own_scales, other_scales):
    near, near_rows, _ = portion.shape
    depth, units = gate_weight.shape[1:]
    out = (GROUP, near * near_rows // GROUP, 2 * units)
    smem = pl.BlockSpec(memory_space=pltpu.SMEM)
    return pl.pallas_call(
        gate_up_kernel,
        grid_spec=pltpu.PrefetchScalarGridSpec(
            num_scalar_prefetch=1,
            grid=(1,),
            in_specs=[
                smem,
                smem,
                whole(portion.shape),
                expert_part(gate_weight.shape),
                expert_part(up_weight.shape),
                whole(other.shape),
            ],
            out_specs=whole(out),
        ),
        out_shape=jax.ShapeDtypeStruct(out, F32),
        compiler_params=pltpu.CompilerParams(vmem_limit_bytes=32 * 1024 * 1024),
        cost_estimate=pl.CostEstimate(
            flops=8 * near * near_rows * depth * units,
            bytes_accessed=near * near_rows * (4 * depth + 8 * units) + 8 * depth * units,
            transcendentals=0,
        ),
        name="gate_up",
    )(core_index, own_scales, other_scales, portion, gate_weight, up_weight, other)


def down_kernel(core_ref, os_ref, rs_ref, h_ref, dw_ref, rw_ref, o_ref):
    near, rows, _ = o_ref.shape
    depth, width = rw_ref.shape
    ks, ns = depth // SB, width // SB
    start = rs_ref.shape[1] - ks * ns
    per = h_ref.shape[0] // near
    for i in range(near):
        for part, scale_ref in enumerate((os_ref, rs_ref)):
            total = None
            for k in range(ks):
                cut = slice(k * SB, (k + 1) * SB)
                hidden = h_ref[i * per : (i + 1) * per, :, cut].reshape(rows, SB)
                weight = dw_ref[0, cut, :] if scale_ref is os_ref else rw_ref[cut, :]
                row = scale_row(lambda c: scale_ref[0, start + k * ns + c], range(ns))
                product = jnp.dot(hidden, weight, preferred_element_type=F32) * row
                total = product if total is None else total + product
            o_ref[i, :, part * width : (part + 1) * width] = total.astype(o_ref.dtype)


def down_project(core_index, hidden, down_weight, other, own_scales, other_scales):
    _, some_rows, depth = hidden.shape
    width = down_weight.shape[2]
    rows = GROUP * some_rows
    out = (NEAR, rows // NEAR, 2 * width)
    smem = pl.BlockSpec(memory_space=pltpu.SMEM)
    return pl.pallas_call(
        down_kernel,
        grid_spec=pltpu.PrefetchScalarGridSpec(
            num_scalar_prefetch=1,
            grid=(1,),
            in_specs=[
                smem,
                smem,
                whole(hidden.shape),
                expert_part(down_weight.shape),
                whole(other.shape),
            ],
            out_specs=whole(out),
        ),
        out_shape=jax.ShapeDtypeStruct(out, BF16),
        compiler_params=pltpu.CompilerParams(vmem_limit_bytes=32 * 1024 * 1024),
        cost_estimate=pl.CostEstimate(
            flops=4 * rows * depth * width,
            bytes_accessed=rows * (2 * depth + 4 * width) + 4 * depth * width,
            transcendentals=0,
        ),
        name="down_project",
    )(core_index, own_scales, other_scales, hidden, down_weight, other)


def shards(
    tokens,
    route_ids,
    route_gates,
    gate_weight,
    up_weight,
    gate_scale,
    up_scale,
    down_weight,
    down_scale,
):
    core = lax.axis_index("core")
    zero = core == 0
    width = tokens.shape[1]
    hidden_width = gate_weight.shape[2]
    near_rows = ZH * CAP
    other_tokens = swap(tokens)
    onehot = dispatch(route_ids)
    own = jnp.where(zero, onehot[:, 0], onehot[:, 1]).astype(BF16)
    slot_rows = [
        jnp.einsum("tc,td->cd", own, part, preferred_element_type=F32).astype(BF16)
        for part in (tokens, other_tokens)
    ]
    slot_rows = jnp.concatenate(slot_rows, axis=1).reshape(8, -1)
    (
        slot_rows,
        onehot,
        route_ids,
        route_gates,
        gate_weight,
        up_weight,
        down_weight,
        gate_scale,
        up_scale,
        down_scale,
    ) = lax.optimization_barrier(
        (
            slot_rows,
            onehot,
            route_ids,
            route_gates,
            gate_weight,
            up_weight,
            down_weight,
            gate_scale,
            up_scale,
            down_scale,
        )
    )
    far = gather(slot_rows, FAR, ZH).reshape(near_rows, 2 * width)

    other = 1 - core
    core_index = jnp.reshape(core, (1,)).astype(jnp.int32)
    sent = jnp.concatenate([pick(gate_weight, other), pick(up_weight, other)], axis=0)
    sent_down, gate_scale, up_scale, down_scale = lax.optimization_barrier(
        (pick(down_weight, other), gate_scale, up_scale, down_scale)
    )
    scales = (gate_scale, up_scale, down_scale)
    own_scales = flat_scales(scales, core)
    other_scales = swap(flat_scales(scales, other))
    other_gate_up = swap(sent)
    other_down = swap(sent_down)
    combine = onehot.astype(F32) * combine_weights(route_ids, route_gates)[:, :, None]
    own_combine = jnp.where(zero, combine[:, 0], combine[:, 1])
    other_combine = jnp.where(zero, combine[:, 1], combine[:, 0])
    (
        far,
        core_index,
        own_scales,
        other_scales,
        other_gate_up,
        other_down,
        own_combine,
        other_combine,
    ) = lax.optimization_barrier(
        (
            far,
            core_index,
            own_scales,
            other_scales,
            other_gate_up,
            other_down,
            own_combine,
            other_combine,
        )
    )
    portion = gather(far, NEIGHBOURS, NEAR)

    partial_sums = gate_up(
        core_index, portion, gate_weight, up_weight, other_gate_up, own_scales, other_scales
    ).astype(jnp.float16)
    received = trade(partial_sums, PLANE)
    summed = jnp.sum(received.astype(F32), axis=0) * (1.0 / SHIFT)
    hidden = (jax.nn.silu(summed[:, :hidden_width]) * summed[:, hidden_width:]).astype(BF16)
    hidden = gather(hidden, PLANE, GROUP)
    down = down_project(core_index, hidden, down_weight, other_down, own_scales, other_scales)
    down = trade(down, NEIGHBOURS)
    down = jnp.sum(down.astype(F32), axis=0).astype(BF16)
    down = trade(down.reshape(ZH, 8, -1), FAR)
    out = jnp.sum(down.astype(F32), axis=0).reshape(CAP, 2 * width)
    given = swap(out[:, width:])
    mixed = jnp.dot(own_combine, out[:, :width], precision=lax.Precision.HIGHEST)
    mixed = mixed + jnp.dot(other_combine, given, precision=lax.Precision.HIGHEST)
    return mixed.astype(BF16)


def solution(mesh):
    parts = Mesh(mesh.devices.reshape(tuple(SIZES.values())), tuple(SIZES))
    in_specs = (
        P(BLK, COL),
        P(BLK, None),
        P(BLK, None),
        P(None, COL, BLK),
        P(None, COL, BLK),
        P(None, COL, BLK),
        P(None, COL, BLK),
        P(None, BLK, COL),
        P(None, BLK, COL),
    )
    return jax.shard_map(
        shards, mesh=parts, in_specs=in_specs, out_specs=P(BLK, COL), check_vma=False
    )
```

```python
import jax
import jax.numpy as jnp
from jax import lax
from jax.experimental import pallas as pl
from jax.experimental.pallas import tpu as pltpu
from jax.sharding import Mesh, PartitionSpec as P

EXPW = 2
CAP = 20
SB = 128
COL = ("ya", "yb", "xh", "core")
BLK = ("za", "zb", "zc", "zl", "xl")
FAR = ("zc", "zb", "za")
NEIGHBOURS = ("xl", "zl")
PLANE = ("xh", "yb", "ya")
SIZES = dict.fromkeys(COL + BLK, 2)
ZH = 2 ** len(FAR)
NEAR = 2 ** len(NEIGHBOURS)
GROUP = 2 ** len(PLANE)
F32 = jnp.float32
BF16 = jnp.bfloat16
SHIFT = 64.0


def matching(route_ids):
    expert_ids = jnp.arange(EXPW, dtype=jnp.int32)
    return route_ids[:, :, None] == expert_ids[None, None, :]


def dispatch(route_ids):
    chosen = jnp.any(matching(route_ids), axis=1)
    slot_index = jnp.cumsum(chosen.astype(jnp.int32), axis=0) - 1
    return chosen[:, :, None] & (
        slot_index[:, :, None] == jnp.arange(CAP, dtype=jnp.int32)[None, None, :]
    )


def combine_weights(route_ids, route_gates):
    return jnp.sum(
        jnp.where(
            matching(route_ids), route_gates[:, :, None], jnp.zeros((), route_gates.dtype)
        ),
        axis=1,
    )


def swap(value):
    return lax.ppermute(value, "core", [(0, 1), (1, 0)])


def trade(value, axes):
    return lax.all_to_all(value, axes, 0, 0, tiled=True)


def gather(value, axes, count):
    return trade(jnp.broadcast_to(value[None], (count,) + value.shape), axes)


def pick(array, index):
    return lax.dynamic_index_in_dim(array, index, 0, keepdims=False)


def flat_scales(scales, expert):
    return jnp.concatenate([pick(scale, expert).reshape(1, -1) for scale in scales], axis=1)


def scale_row(read, blocks):
    return jnp.concatenate([jnp.full((1, SB), read(block), F32) for block in blocks], axis=1)


def gate_up_kernel(core_ref, os_ref, rs_ref, x_ref, gw_ref, uw_ref, rw_ref, o_ref):
    near = x_ref.shape[0]
    depth, units = gw_ref.shape[1:]
    ks, ns = depth // SB, units // SB
    chunk = 2 * SB
    per = o_ref.shape[0] // near
    for i in range(near):
        for which, own_weight in enumerate((gw_ref, uw_ref)):
            for n in range(units // chunk):
                columns = slice(n * chunk, (n + 1) * chunk)
                blocks = (2 * n, 2 * n + 1)
                total = None
                for part, scale_ref in enumerate((os_ref, rs_ref)):
                    for k in range(ks):
                        cut = slice(k * SB, (k + 1) * SB)
                        start = part * depth + k * SB
                        rows = x_ref[i, :, start : start + SB]
                        if scale_ref is os_ref:
                            weight = own_weight[0, cut, columns]
                        else:
                            first = which * depth + k * SB
                            weight = rw_ref[first : first + SB, columns]
                        place = (which * ks + k) * ns
                        row = scale_row(lambda c: scale_ref[0, place + c] * SHIFT, blocks)
                        product = jnp.dot(rows, weight, preferred_element_type=F32) * row
                        total = product if total is None else total + product
                left = which * units + n * chunk
                o_ref[i * per : (i + 1) * per, :, left : left + chunk] = total.reshape(
                    (per, o_ref.shape[1], chunk)
                )


def whole(shape):
    return pl.BlockSpec(shape, lambda i, c: (0,) * len(shape))


def expert_part(shape):
    return pl.BlockSpec((1,) + shape[1:], lambda i, c: (c[0],) + (0,) * (len(shape) - 1))


def gate_up(core_index, portion, gate_weight, up_weight, other, own_scales, other_scales):
    near, near_rows, _ = portion.shape
    depth, units = gate_weight.shape[1:]
    out = (GROUP, near * near_rows // GROUP, 2 * units)
    smem = pl.BlockSpec(memory_space=pltpu.SMEM)
    return pl.pallas_call(
        gate_up_kernel,
        grid_spec=pltpu.PrefetchScalarGridSpec(
            num_scalar_prefetch=1,
            grid=(1,),
            in_specs=[
                smem,
                smem,
                whole(portion.shape),
                expert_part(gate_weight.shape),
                expert_part(up_weight.shape),
                whole(other.shape),
            ],
            out_specs=whole(out),
        ),
        out_shape=jax.ShapeDtypeStruct(out, F32),
        compiler_params=pltpu.CompilerParams(vmem_limit_bytes=32 * 1024 * 1024),
        cost_estimate=pl.CostEstimate(
            flops=8 * near * near_rows * depth * units,
            bytes_accessed=near * near_rows * (4 * depth + 8 * units) + 8 * depth * units,
            transcendentals=0,
        ),
        name="gate_up",
    )(core_index, own_scales, other_scales, portion, gate_weight, up_weight, other)


def down_kernel(core_ref, os_ref, rs_ref, h_ref, dw_ref, rw_ref, o_ref):
    near, rows, _ = o_ref.shape
    depth, width = rw_ref.shape
    ks, ns = depth // SB, width // SB
    start = rs_ref.shape[1] - ks * ns
    per = h_ref.shape[0] // near
    for i in range(near):
        for part, scale_ref in enumerate((os_ref, rs_ref)):
            total = None
            for k in range(ks):
                cut = slice(k * SB, (k + 1) * SB)
                hidden = h_ref[i * per : (i + 1) * per, :, cut].reshape(rows, SB)
                weight = dw_ref[0, cut, :] if scale_ref is os_ref else rw_ref[cut, :]
                row = scale_row(lambda c: scale_ref[0, start + k * ns + c], range(ns))
                product = jnp.dot(hidden, weight, preferred_element_type=F32) * row
                total = product if total is None else total + product
            o_ref[i, :, part * width : (part + 1) * width] = total.astype(o_ref.dtype)


def down_project(core_index, hidden, down_weight, other, own_scales, other_scales):
    _, some_rows, depth = hidden.shape
    width = down_weight.shape[2]
    rows = GROUP * some_rows
    out = (NEAR, rows // NEAR, 2 * width)
    smem = pl.BlockSpec(memory_space=pltpu.SMEM)
    return pl.pallas_call(
        down_kernel,
        grid_spec=pltpu.PrefetchScalarGridSpec(
            num_scalar_prefetch=1,
            grid=(1,),
            in_specs=[
                smem,
                smem,
                whole(hidden.shape),
                expert_part(down_weight.shape),
                whole(other.shape),
            ],
            out_specs=whole(out),
        ),
        out_shape=jax.ShapeDtypeStruct(out, BF16),
        compiler_params=pltpu.CompilerParams(vmem_limit_bytes=32 * 1024 * 1024),
        cost_estimate=pl.CostEstimate(
            flops=4 * rows * depth * width,
            bytes_accessed=rows * (2 * depth + 4 * width) + 4 * depth * width,
            transcendentals=0,
        ),
        name="down_project",
    )(core_index, own_scales, other_scales, hidden, down_weight, other)


def shards(
    tokens,
    route_ids,
    route_gates,
    gate_weight,
    up_weight,
    gate_scale,
    up_scale,
    down_weight,
    down_scale,
):
    core = lax.axis_index("core")
    zero = core == 0
    width = tokens.shape[1]
    hidden_width = gate_weight.shape[2]
    near_rows = ZH * CAP
    other_tokens = swap(tokens)
    onehot = dispatch(route_ids)
    own = jnp.where(zero, onehot[:, 0], onehot[:, 1]).astype(BF16)
    both_tokens = jnp.concatenate([tokens, other_tokens], axis=1)
    slot_rows = jnp.einsum("tc,td->cd", own, both_tokens, preferred_element_type=F32)
    slot_rows = slot_rows.astype(BF16).reshape(8, -1)
    (
        slot_rows,
        onehot,
        route_ids,
        route_gates,
        gate_weight,
        up_weight,
        down_weight,
        gate_scale,
        up_scale,
        down_scale,
    ) = lax.optimization_barrier(
        (
            slot_rows,
            onehot,
            route_ids,
            route_gates,
            gate_weight,
            up_weight,
            down_weight,
            gate_scale,
            up_scale,
            down_scale,
        )
    )
    far = gather(slot_rows, FAR, ZH).reshape(near_rows, 2 * width)

    other = 1 - core
    core_index = jnp.reshape(core, (1,)).astype(jnp.int32)
    sent = jnp.concatenate([pick(gate_weight, other), pick(up_weight, other)], axis=0)
    sent_down, gate_scale, up_scale, down_scale = lax.optimization_barrier(
        (pick(down_weight, other), gate_scale, up_scale, down_scale)
    )
    scales = (gate_scale, up_scale, down_scale)
    own_scales = flat_scales(scales, core)
    other_scales = swap(flat_scales(scales, other))
    other_gate_up = swap(sent)
    other_down = swap(sent_down)
    combine = onehot.astype(F32) * combine_weights(route_ids, route_gates)[:, :, None]
    own_combine = jnp.where(zero, combine[:, 0], combine[:, 1])
    other_combine = jnp.where(zero, combine[:, 1], combine[:, 0])
    (
        far,
        core_index,
        own_scales,
        other_scales,
        other_gate_up,
        other_down,
        own_combine,
        other_combine,
    ) = lax.optimization_barrier(
        (
            far,
            core_index,
            own_scales,
            other_scales,
            other_gate_up,
            other_down,
            own_combine,
            other_combine,
        )
    )
    portion = gather(far, NEIGHBOURS, NEAR)

    partial_sums = gate_up(
        core_index, portion, gate_weight, up_weight, other_gate_up, own_scales, other_scales
    ).astype(jnp.float16)
    received = trade(partial_sums, PLANE)
    summed = jnp.sum(received.astype(F32), axis=0) * (1.0 / SHIFT)
    hidden = (jax.nn.silu(summed[:, :hidden_width]) * summed[:, hidden_width:]).astype(BF16)
    hidden = gather(hidden, PLANE, GROUP)
    down = down_project(core_index, hidden, down_weight, other_down, own_scales, other_scales)
    down = trade(down, NEIGHBOURS)
    down = jnp.sum(down.astype(F32), axis=0).astype(BF16)
    down = trade(down.reshape(ZH, 8, -1), FAR)
    out = jnp.sum(down.astype(F32), axis=0).reshape(CAP, 2 * width)
    given = swap(out[:, width:])
    mixed = jnp.dot(own_combine, out[:, :width], precision=lax.Precision.HIGHEST)
    mixed = mixed + jnp.dot(other_combine, given, precision=lax.Precision.HIGHEST)
    return mixed.astype(BF16)


def solution(mesh):
    parts = Mesh(mesh.devices.reshape(tuple(SIZES.values())), tuple(SIZES))
    in_specs = (
        P(BLK, COL),
        P(BLK, None),
        P(BLK, None),
        P(None, COL, BLK),
        P(None, COL, BLK),
        P(None, COL, BLK),
        P(None, COL, BLK),
        P(None, BLK, COL),
        P(None, BLK, COL),
    )
    return jax.shard_map(
        shards, mesh=parts, in_specs=in_specs, out_specs=P(BLK, COL), check_vma=False
    )
```
